128 devices in a mesh: expert: 32 (over x, z, core), dp: 4 (over y).
Axes of the slice: x: 4, y: 4, z: 4, core: 2. Of those that a mesh axis runs over, the one named last changes fastest.
Arguments:
- tokens: bfloat16 [16384, 4096], P(('dp', 'expert')), parts along dimension 0, may hold values from -6 to 6
- expert_ids: int32 [16384, 8], P(('dp', 'expert')), parts along dimension 0, may hold values from 0 to 31, all different within a row; in each aligned block of 128 rows (0 to 127, 128 to 255, ...) at most 48 rows name the same one
- gate_weights: bfloat16 [16384, 8], P(('dp', 'expert')), parts along dimension 0, may hold values from 0.049804688 to 1
- expert_in: bfloat16 [32, 4096, 1536], P('expert'), may hold values from -0.09375 to 0.09375
- expert_out: bfloat16 [32, 768, 4096], P('expert'), may hold values from -0.21875 to 0.21875
Outputs:
- combined: bfloat16 [16384, 4096], P(('dp', 'expert')), parts along dimension 0
The draws below stay inside these ranges and needn't reach their ends.
There are 4 independent parts, one for each index of `dp`. The reference program is written for one: setup_inputs(seed, part) draws one part's arguments, and reference() takes and returns one part's arrays. A program takes and returns all parts, laid end to end along the dimension named above; an argument that names none is the same for every part. Nothing has to cross between parts.
Inputs may be any that keep to these rules, and one draw needn't show every extreme that they name: `expert_ids`: each row names 8 different experts. Within the rows of one device (aligned blocks of 128 tokens) no expert is named by more than 48 rows, and in every draw some expert is named by exactly 48 rows of some device.
All inputs are finite; a program needn't handle non-finite values.
Results may differ from the reference program's by a relative error of at most 0.0057.
Values may be sent and summed in bfloat16 or wider, within the bound.
No kernel may reach another device: no remote copies, remote signals or barrier semaphores. Data moves between devices by JAX's collectives and lax.ppermute only.
A program may use at most 192 MiB of HBM per device.

```python
import math
import jax
import jax.numpy as jnp
import numpy as np
from jax import lax

D = 4096
F = 768
EXPERTS = 32
TOPK = 8
TOK_DEV = 128
CAP = 48
TOKENS = 4096
N_EXPERT = 32


def block_levels(own_key, dims, shards, smallest, top_value):
    factor_of, own = 1.0, jax.random.fold_in(own_key, 6)
    for dim, blocks in shards:
        steps = jnp.exp(jax.random.uniform(jax.random.fold_in(own, dim), (blocks,), jnp.float32, smallest / len(shards), top_value / len(shards)))
        factor_of = factor_of * jnp.repeat(steps, dims[dim] // blocks).reshape([-1 if axis == dim else 1 for axis in range(len(dims))])
    return factor_of


def routed_block(rng, own, number, rows, amount, top, most, lean):
    order = jax.random.permutation(rng, amount)
    packed, ordinary = portions_of(amount, rows * top, most, lean, True), portions_of(amount, rows * top, most, lean, False)
    places = jnp.arange(amount)

    def named(sizes, turn):
        used = int((sizes > 0).sum())
        fixed = max(1, used // 4)
        shifted = fixed + (places - fixed + turn * (used - fixed)) % max(1, amount - fixed)
        return jnp.zeros((amount,), jnp.int32).at[order[jnp.where(places < fixed, places, shifted)]].set(jnp.asarray(sizes, jnp.int32))

    sizes = jnp.where(number % 4 == 0, named(packed, number // 4), named(ordinary, number - number // 4 - 1))
    mixed = jax.random.permutation(jax.random.fold_in(own, 3), amount)
    giver, receiver = mixed[0:amount // 2 * 2:2], mixed[1:amount // 2 * 2:2]
    margin = jnp.minimum(sizes[giver] - 1, most - sizes[receiver]) // 2
    margin = jnp.where((giver == order[0]) | (receiver == order[0]) | (sizes[receiver] == 0), 0, jnp.maximum(margin, 0))
    shifted = jax.random.randint(jax.random.fold_in(own, 4), (amount // 2,), 0, 1 << 20) % (margin + 1)
    sizes = sizes.at[giver].add(-shifted).at[receiver].add(shifted)
    items = jnp.searchsorted(jnp.cumsum(sizes), jnp.arange(rows * top), side="right").astype(jnp.int32)
    grid = items.reshape(top, rows).T
    grid = grid[jax.random.permutation(jax.random.fold_in(own, 1), rows)]
    turn = jax.random.randint(jax.random.fold_in(own, 2), (rows, 1), 0, top)
    return jnp.take_along_axis(grid, (jnp.arange(top)[None, :] + turn) % top, axis=1)


def portions_of(amount, total, reach, skew, full):
    portions = [(1 << 20) // math.isqrt(standing ** skew) + 1 for standing in range(1, amount + 1)]
    largest = reach if full else min(reach, max(-(-total // amount), total * portions[0] // sum(portions)))
    least = 1 if total - largest >= amount - 1 else 0
    given, rest = [largest] + [least] * (amount - 1), total - largest - least * (amount - 1)
    while rest > 0:
        free = [i for i in range(1, amount) if given[i] < largest] or [i for i in range(1, amount) if given[i] < reach]
        pool, left = sum([portions[i] for i in free]), rest
        for i in free:
            addition = min(reach - given[i], max(1, left * portions[i] // pool), rest)
            given[i] = given[i] + addition
            rest = rest - addition
    return np.array(given)


def normal_values(rng, extent, width, most, cuts=(), held_as=jnp.bfloat16):
    result = jax.random.normal(rng, extent, jnp.float32) * width
    if len(cuts) > 0:
        result = block_levels(rng, extent, cuts, -0.22, 0.18) * result
    return jnp.clip(result, min=-most, max=most).astype(held_as)


def setup_inputs(seed: int = 0, part: int = 0) -> dict:
    streams_of = jax.random.split(jax.random.key(seed), 6)
    part_splits = jax.random.split(jax.random.fold_in(streams_of[5], part), 6)
    tokens = normal_values(part_splits[0], (TOKENS, D), 1.0, 6.0, ((0, 32),))
    expert_ids_keys = jax.random.split(jax.random.fold_in(part_splits[1], 1), TOKENS // TOK_DEV)
    expert_ids_turns = jax.random.permutation(jax.random.fold_in(part_splits[1], 3), TOKENS // TOK_DEV)
    expert_ids = jax.vmap(lambda own, number: routed_block(jax.random.fold_in(part_splits[1], 2), own, number, TOK_DEV, EXPERTS, TOPK, CAP, 2))(expert_ids_keys, expert_ids_turns).reshape((TOKENS, TOPK))
    gate_weights = jnp.clip(jnp.exp(math.log(1.0) - 2.9996462 * jax.random.uniform(part_splits[2], (TOKENS, TOPK), jnp.float32) ** block_levels(part_splits[2], (TOKENS, TOPK), ((0, 32),), -0.2, 0.2)), 0.049804688, 1.0).astype(jnp.bfloat16)
    expert_in = normal_values(streams_of[3], (EXPERTS, D, 2 * F), D ** -0.5, 0.09375, ((0, 32),))
    expert_out = normal_values(streams_of[4], (EXPERTS, F, D), F ** -0.5, 0.21875, ((0, 32),))
    return dict(tokens=tokens, expert_ids=expert_ids, gate_weights=gate_weights, expert_in=expert_in, expert_out=expert_out)


def expert_math(inputs, gains, first_weights, second_weights):
    hidden = jnp.dot(inputs, first_weights, preferred_element_type=jnp.float32)
    half_width = first_weights.shape[1] // 2
    activation = (jax.nn.silu(hidden[:, :half_width]) * hidden[:, half_width:]).astype(jnp.bfloat16)
    projected = jnp.dot(activation, second_weights, preferred_element_type=jnp.float32)
    return (gains[:, None] * projected).astype(jnp.bfloat16)


def reference(tokens, expert_ids, gate_weights, expert_in, expert_out):
    total_rows = tokens.shape[0]
    gates_wide = gate_weights.astype(jnp.float32)
    limit = N_EXPERT * CAP

    def one_expert(totals, inputs):
        first_weights, second_weights, expert_index = inputs
        hits = expert_ids == expert_index
        chosen = jnp.nonzero(jnp.any(hits, axis=1), size=limit, fill_value=total_rows)[0].astype(jnp.int32)
        token_gains = jnp.sum(jnp.where(hits, gates_wide, jnp.zeros_like(gates_wide)), axis=1)
        picked = jnp.take(tokens, chosen, axis=0, mode="fill", fill_value=0)
        picked_gains = jnp.take(token_gains, chosen, axis=0, mode="fill", fill_value=0)
        weighted = expert_math(picked, picked_gains, first_weights, second_weights)
        totals = totals.at[chosen].add(weighted.astype(jnp.float32), mode="drop")
        return totals, None

    start = jnp.zeros(tokens.shape, jnp.float32)
    totals, unused = lax.scan(one_expert, start, (expert_in, expert_out, jnp.arange(EXPERTS, dtype=jnp.int32)))
    return totals.astype(jnp.bfloat16)
```

```python
import jax
import jax.numpy as jnp
from jax import lax
from jax.experimental import pallas as pl
from jax.experimental.pallas import tpu as pltpu
from jax.sharding import PartitionSpec as P

SIDE = 4
CAP = 48
ROWS = 128
HALF = 64
COLS = 1024
FT = 256
VMEM = 56 * 1024 * 1024
OFFSETS = (0, -1, 1, 2)


def chip_index(x, z, core):
    return (x % SIDE) * (2 * SIDE) + (z % SIDE) * 2 + core


def ring_pairs(step, second):
    pairs = []
    for i in range(2 * SIDE * SIDE):
        x, z, core = i // 8, (i // 2) % 4, i % 2
        along_x = (core == 0) != second
        pairs.append((i, chip_index(x + step, z, core) if along_x else chip_index(x, z + step, core)))
    return pairs


SWAP = [(i, i ^ 1) for i in range(2 * SIDE * SIDE)]


def hop(value, step, second):
    return lax.ppermute(value, "expert", ring_pairs(step, second))


def swap(value):
    return lax.ppermute(value, "expert", SWAP)


def shifted(table, start, axis):
    return lax.dynamic_slice_in_dim(jnp.concatenate([table, table], axis=axis), start, SIDE, axis)


def stream_part(table, core, same, i):
    along_x = jnp.stack([table[i % SIDE, j % SIDE, 0] for j in OFFSETS])
    along_z = jnp.stack([table[j % SIDE, i % SIDE, 1] for j in OFFSETS])
    return jnp.where((core == 0) == same, along_x, along_z)


def params(vmem=VMEM):
    return pltpu.CompilerParams(vmem_limit_bytes=vmem)


def select_kernel(pos_ref, own_ref, left_ref, right_ref, far_a_ref, far_b_ref, mine_ref, other_ref):
    slots = lax.broadcasted_iota(jnp.int32, (CAP, ROWS), 0)
    for b, refs in enumerate(((own_ref,), (left_ref,), (right_ref,), (far_a_ref, far_b_ref))):
        for k, out in enumerate((mine_ref, other_ref)):
            pick = jnp.where(pos_ref[2 * b + k : 2 * b + k + 1, :] == slots, 1.0, 0.0).astype(jnp.bfloat16)
            if len(refs) == 1:
                rows = jnp.dot(pick, refs[0][...], preferred_element_type=jnp.float32)
            else:
                rows = jnp.dot(pick[:, :HALF], refs[0][...], preferred_element_type=jnp.float32)
                rows += jnp.dot(pick[:, HALF:], refs[1][...], preferred_element_type=jnp.float32)
            out[b * CAP : (b + 1) * CAP, :] = rows.astype(jnp.bfloat16)


def select_rows(pos, blocks):
    width = blocks[0].shape[1]
    spec = lambda rows: pl.BlockSpec((rows, COLS), lambda n: (0, n))
    out = jax.ShapeDtypeStruct((4 * CAP, width), jnp.bfloat16)
    return pl.pallas_call(
        select_kernel,
        grid=(width // COLS,),
        in_specs=[pl.BlockSpec((8, ROWS), lambda n: (0, 0))] + [spec(b.shape[0]) for b in blocks],
        out_specs=[spec(4 * CAP)] * 2,
        out_shape=[out, out],
        compiler_params=params(),
        cost_estimate=pl.CostEstimate(flops=2 * 8 * CAP * ROWS * width, bytes_accessed=7 * 1024 * 1024, transcendentals=0),
    )(pos, *blocks)


def expert_kernel(mine_ref, other_ref, gain_ref, gate_ref, up_ref, down_ref, mine_out, other_out, rows_ref, total_ref):
    step = pl.program_id(0)
    half = mine_ref.shape[0]

    @pl.when(step == 0)
    def _():
        rows_ref[:half, :] = mine_ref[...]
        rows_ref[half:, :] = other_ref[...]

    rows = rows_ref[...]
    first = jnp.dot(rows, gate_ref[...], preferred_element_type=jnp.float32)
    second = jnp.dot(rows, up_ref[...], preferred_element_type=jnp.float32)
    activation = (first / (1.0 + jnp.exp(-first)) * second).astype(jnp.bfloat16)
    for n in range(0, down_ref.shape[1], COLS):
        part = jnp.dot(activation, down_ref[:, n : n + COLS], preferred_element_type=jnp.float32)

        @pl.when(step == 0)
        def _():
            total_ref[:, n : n + COLS] = part

        @pl.when(step == 1)
        def _():
            total_ref[:, n : n + COLS] += part

        @pl.when(step == 2)
        def _():
            weighted = ((total_ref[:, n : n + COLS] + part) * gain_ref[...]).astype(jnp.bfloat16)
            mine_out[:, n : n + COLS] = weighted[:half]
            other_out[:, n : n + COLS] = weighted[half:]


def expert_rows(mine, other, gains, expert_in, expert_out):
    count, width = mine.shape
    hidden = expert_out.shape[0]
    steps = hidden // FT
    whole = pl.BlockSpec((count, width), lambda f: (0, 0))
    out = jax.ShapeDtypeStruct((count, width), jnp.bfloat16)
    return pl.pallas_call(
        expert_kernel,
        grid=(steps,),
        in_specs=[
            whole,
            whole,
            pl.BlockSpec((2 * count, 1), lambda f: (0, 0)),
            pl.BlockSpec((width, FT), lambda f: (0, f)),
            pl.BlockSpec((width, FT), lambda f: (0, f + steps)),
            pl.BlockSpec((FT, width), lambda f: (f, 0)),
        ],
        out_specs=[whole, whole],
        out_shape=[out, out],
        scratch_shapes=[
            pltpu.VMEM((2 * count, width), jnp.bfloat16),
            pltpu.VMEM((2 * count, width), jnp.float32),
        ],
        compiler_params=params(),
        cost_estimate=pl.CostEstimate(
            flops=2 * 2 * count * width * hidden * 3, bytes_accessed=30 * 1024 * 1024, transcendentals=2 * count * hidden
        ),
    )(mine, other, gains, expert_in, expert_in, expert_out)


def spread_kernel(plan, pos_ref, mine_ref, other_ref, *refs):
    slots = lax.broadcasted_iota(jnp.int32, (ROWS, CAP), 1)
    taken = 0
    given = sum(len(addends) for _, addends, _ in plan)
    for b, addends, outs in plan:
        total = None
        for k, source in enumerate((mine_ref, other_ref)):
            put = jnp.where(pos_ref[:, 2 * b + k : 2 * b + k + 1] == slots, 1.0, 0.0).astype(jnp.bfloat16)
            part = jnp.dot(put, source[b * CAP : (b + 1) * CAP, :], preferred_element_type=jnp.float32)
            total = part if total is None else total + part
        top, bottom = total[:HALF], total[HALF:]
        for start, rows in addends:
            extra = refs[taken][...].astype(jnp.float32)
            taken += 1
            if rows == ROWS:
                top, bottom = top + extra[:HALF], bottom + extra[HALF:]
            elif start == 0:
                top = top + extra
            else:
                bottom = bottom + extra
        for start, rows in outs:
            out = refs[given]
            given += 1
            if rows == ROWS:
                out[:HALF, :] = top.astype(jnp.bfloat16)
                out[HALF:, :] = bottom.astype(jnp.bfloat16)
            else:
                out[...] = (top if start == 0 else bottom).astype(jnp.bfloat16)


def spread_rows(pos, mine, other, blocks):
    width = mine.shape[1]
    spec = lambda rows: pl.BlockSpec((rows, COLS), lambda n: (0, n))
    plan, extras, outs = [], [], []
    for b, addends, given in blocks:
        plan.append((b, [(start, a.shape[0]) for start, a in addends], given))
        extras += [a for _, a in addends]
        outs += [rows for _, rows in given]

    def body(*refs):
        spread_kernel(plan, *refs)

    return pl.pallas_call(
        body,
        grid=(width // COLS,),
        in_specs=[pl.BlockSpec((ROWS, 8), lambda n: (0, 0)), spec(4 * CAP), spec(4 * CAP)] + [spec(a.shape[0]) for a in extras],
        out_specs=[spec(rows) for rows in outs],
        out_shape=[jax.ShapeDtypeStruct((rows, width), jnp.bfloat16) for rows in outs],
        compiler_params=params(),
        cost_estimate=pl.CostEstimate(
            flops=2 * 2 * CAP * ROWS * width * len(blocks), bytes_accessed=3 * 1024 * 1024 * len(blocks), transcendentals=0
        ),
    )(pos, mine, other, *extras)


def routing(expert_ids, gate_weights, me, x, z):
    table = jnp.concatenate([expert_ids.T.astype(jnp.bfloat16), gate_weights.T], axis=0)
    table = lax.all_gather(table, "expert", axis=0, tiled=False)
    table = shifted(shifted(table.reshape(SIDE, SIDE, 2, 16, ROWS), x, 0), z, 1).reshape(2 * SIDE * SIDE, 16, ROWS)
    ids, gates = table[:, :8, :], table[:, 8:, :].astype(jnp.float32)
    both = jnp.stack([me, me ^ 1]).astype(jnp.bfloat16)
    match = ids[:, None, :, :] == both[None, :, None, None]
    hit = jnp.any(match, axis=2)
    gate = jnp.sum(jnp.where(match, gates[:, None, :, :], 0.0), axis=2)
    before = (jnp.arange(ROWS)[:, None] < jnp.arange(ROWS)[None, :]).astype(jnp.bfloat16)
    rank = jnp.einsum("bet,ts->bes", hit.astype(jnp.bfloat16), before, preferred_element_type=jnp.float32)
    slot = jnp.where(hit, rank.astype(jnp.int32), -1)
    is_slot = slot[:, 0, None, :] == jnp.arange(CAP, dtype=jnp.int32)[None, :, None]
    gains = jnp.sum(jnp.where(is_slot, gate[:, 0, None, :], 0.0), axis=2)
    return slot.reshape(SIDE, SIDE, 2, 2, ROWS), gains.reshape(SIDE, SIDE, 2, CAP)


def gather_ring(block, second):
    left, right = hop(block, 1, second), hop(block, -1, second)
    far_a, far_b = hop(left[:HALF], 1, second), hop(right[HALF:], -1, second)
    return block, left, right, far_a, far_b


def on_device(tokens, expert_ids, gate_weights, expert_in, expert_out):
    me = lax.axis_index("expert")
    core, x, z = me % 2, me // 8, (me // 2) % 4
    first_weights, second_weights = expert_in[0], expert_out[0]
    slot, gains = routing(expert_ids, gate_weights, me, x, z)

    own, left, right, far_a, far_b = gather_ring(tokens, False)
    starts = (own, left, right, jnp.concatenate([far_a, far_b], axis=0))
    results = []
    for i, start in zip(OFFSETS, starts):
        pos = stream_part(slot, core, True, i).reshape(8, ROWS)
        pos_column = pos.T
        gain = jnp.concatenate([stream_part(gains, core, same, i) for same in (True, False)], axis=0).reshape(8 * CAP, 1)
        mine, other = select_rows(pos, gather_ring(start, True))
        arrived = swap(other)
        mine_out, other_out = expert_rows(mine, arrived, gain, first_weights, second_weights)
        back = swap(other_out)
        results.append((pos_column, mine_out, back))

    def reduce_second(n):
        pos, mine, back = results[n]
        top, bottom = spread_rows(pos, mine, back, [(3, [], [(0, HALF), (HALF, HALF)])])
        from_left, from_right = hop(top, 1, True), hop(bottom, -1, True)
        to_right, to_left = spread_rows(
            pos, mine, back, [(2, [(0, from_left)], [(0, ROWS)]), (1, [(HALF, from_right)], [(0, ROWS)])]
        )
        return hop(to_right, 1, True), hop(to_left, -1, True)

    a0, b0 = reduce_second(0)
    a3, b3 = reduce_second(3)
    top, bottom = spread_rows(*results[3], [(0, [(0, a3), (0, b3)], [(0, HALF), (HALF, HALF)])])
    from_left, from_right = hop(top, 1, False), hop(bottom, -1, False)
    a2, b2 = reduce_second(2)
    (to_right,) = spread_rows(*results[2], [(0, [(0, a2), (0, b2), (0, from_left)], [(0, ROWS)])])
    a1, b1 = reduce_second(1)
    (to_left,) = spread_rows(*results[1], [(0, [(0, a1), (0, b1), (HALF, from_right)], [(0, ROWS)])])
    c, d = hop(to_right, 1, False), hop(to_left, -1, False)
    (out,) = spread_rows(*results[0], [(0, [(0, a0), (0, b0), (0, c), (0, d)], [(0, ROWS)])])
    return out


def solution(mesh):
    placed = (
        P(("dp", "expert"), None),
        P(("dp", "expert"), None),
        P(("dp", "expert"), None),
        P("expert", None, None),
        P("expert", None, None),
    )
    return jax.shard_map(
        on_device, mesh=mesh, in_specs=placed, out_specs=P(("dp", "expert"), None), check_vma=False
    )
```

```python
import jax
import jax.numpy as jnp
from jax import lax
from jax.experimental import pallas as pl
from jax.experimental.pallas import tpu as pltpu
from jax.sharding import PartitionSpec as P

SIDE = 4
CAP = 48
ROWS = 128
HALF = 64
COLS = 2048
NT = 1024
GATHERED = 128
FT = 256
MIB = 1024 * 1024


def chip_index(x, z, core):
    return (x % SIDE) * (2 * SIDE) + (z % SIDE) * 2 + core


def ring_pairs(step, second):
    pairs = []
    for i in range(2 * SIDE * SIDE):
        x, z, core = i // 8, (i // 2) % 4, i % 2
        along_x = (core == 0) != second
        pairs.append((i, chip_index(x + step, z, core) if along_x else chip_index(x, z + step, core)))
    return pairs


SWAP = [(i, i ^ 1) for i in range(2 * SIDE * SIDE)]


def hop(value, step, second):
    return lax.ppermute(value, "expert", ring_pairs(step, second))


def swap(value):
    return lax.ppermute(value, "expert", SWAP)


def shifted(table, start, axis):
    return lax.dynamic_slice_in_dim(jnp.concatenate([table, table], axis=axis), start, SIDE, axis)


SHORT = pl.CostEstimate(flops=1000, bytes_accessed=1000, transcendentals=0)


LONG = pl.CostEstimate(flops=10**12, bytes_accessed=10**9, transcendentals=0)


def params(vmem):
    return pltpu.CompilerParams(vmem_limit_bytes=vmem)


def select_rows(pos, places, arrays):
    width = arrays[0].shape[1]
    count = len(places) * CAP

    def kernel(pos_ref, *refs):
        arrays, (mine_ref, other_ref) = refs[:-2], refs[-2:]
        slots = lax.broadcasted_iota(jnp.int32, (2 * CAP, ROWS), 0)
        for b, parts in enumerate(places):
            first, second = pos_ref[2 * b : 2 * b + 1, :], pos_ref[2 * b + 1 : 2 * b + 2, :]
            slot = jnp.where(slots < CAP, first, jnp.where(second < 0, -1, second + CAP))
            pick = jnp.where(slot == slots, 1.0, 0.0).astype(jnp.bfloat16)
            rows = None
            for n, start, at, size in parts:
                part = jnp.dot(pick[:, at : at + size], arrays[n][start : start + size, :], preferred_element_type=jnp.float32)
                rows = part if rows is None else rows + part
            mine_ref[b * CAP : (b + 1) * CAP, :] = rows[:CAP].astype(jnp.bfloat16)
            other_ref[b * CAP : (b + 1) * CAP, :] = rows[CAP:].astype(jnp.bfloat16)

    spec = lambda rows: pl.BlockSpec((rows, COLS), lambda n: (0, n))
    out = jax.ShapeDtypeStruct((count, width), jnp.bfloat16)
    return pl.pallas_call(
        kernel,
        grid=(width // COLS,),
        in_specs=[pl.BlockSpec(pos.shape, lambda n: (0, 0))] + [spec(a.shape[0]) for a in arrays],
        out_specs=[spec(count)] * 2,
        out_shape=[out, out],
        compiler_params=params(24 * MIB),
        cost_estimate=SHORT,
    )(pos, *arrays)


def expert_kernel(steps, mine_ref, other_ref, gain_ref, gate_ref, up_ref, down_ref, mine_out, other_out, rows_ref, act_ref):
    step = pl.program_id(0)
    half = mine_ref.shape[0]

    @pl.when(step == 0)
    def _():
        rows_ref[:half, :] = mine_ref[...]
        rows_ref[half:, :] = other_ref[...]

    for f in range(steps):

        @pl.when(step == f)
        def _():
            rows = rows_ref[...]
            first = jnp.dot(rows, gate_ref[...], preferred_element_type=jnp.float32)
            second = jnp.dot(rows, up_ref[...], preferred_element_type=jnp.float32)
            act_ref[:, f * FT : (f + 1) * FT] = (first / (1.0 + jnp.exp(-first)) * second).astype(jnp.bfloat16)

    @pl.when(step >= steps)
    def _():
        part = jnp.dot(act_ref[...], down_ref[...], preferred_element_type=jnp.float32)
        weighted = (part * gain_ref[...]).astype(jnp.bfloat16)
        mine_out[...] = weighted[:half]
        other_out[...] = weighted[half:]


def expert_rows(mine, other, gains, expert_in, expert_out):
    count, width = mine.shape
    hidden = expert_out.shape[0]
    steps = hidden // FT
    whole = pl.BlockSpec((count, width), lambda s: (0, 0), pipeline_mode=pl.Buffered(1))
    late = lambda s: jnp.maximum(s - steps, 0)
    early = lambda s: jnp.minimum(s, steps - 1)
    out = jax.ShapeDtypeStruct((count, width), jnp.bfloat16)

    def body(*refs):
        expert_kernel(steps, *refs)

    return pl.pallas_call(
        body,
        grid=(steps + width // NT,),
        in_specs=[
            whole,
            whole,
            pl.BlockSpec((2 * count, 1), lambda s: (0, 0)),
            pl.BlockSpec((width, FT), lambda s: (0, early(s))),
            pl.BlockSpec((width, FT), lambda s: (0, early(s) + steps)),
            pl.BlockSpec((hidden, NT), lambda s: (0, late(s))),
        ],
        out_specs=[pl.BlockSpec((count, NT), lambda s: (0, late(s)))] * 2,
        out_shape=[out, out],
        scratch_shapes=[
            pltpu.VMEM((2 * count, width), jnp.bfloat16),
            pltpu.VMEM((2 * count, hidden), jnp.bfloat16),
        ],
        compiler_params=params(44 * MIB),
        cost_estimate=SHORT,
    )(mine, other, gains, expert_in, expert_in, expert_out)


def spread_rows(pos, mine, other, blocks, sizes):
    width = mine.shape[1]
    extras = [addend for _, addends, _ in blocks for addend in addends]
    plan = [(b, [(rows, at) for _, _, rows, at in addends], puts) for b, addends, puts in blocks]

    def kernel(pos_ref, *refs):
        slots = lax.broadcasted_iota(jnp.int32, (ROWS, 2 * CAP), 1)
        sources, refs = refs[: 2 * len(plan)], refs[2 * len(plan) :]
        extra_refs, outs = refs[: len(extras)], refs[len(extras) :]
        taken = 0
        for n, (b, addends, puts) in enumerate(plan):
            first, second = pos_ref[:, 2 * b : 2 * b + 1], pos_ref[:, 2 * b + 1 : 2 * b + 2]
            slot = jnp.where(slots < CAP, first, jnp.where(second < 0, -1, second + CAP))
            put = jnp.where(slot == slots, 1.0, 0.0).astype(jnp.bfloat16)
            rows = jnp.concatenate([sources[2 * n][...], sources[2 * n + 1][...]], axis=0)
            total = jnp.dot(put, rows, preferred_element_type=jnp.float32)
            top, bottom = total[:HALF], total[HALF:]
            for size, at in addends:
                extra = extra_refs[taken][...].astype(jnp.float32)
                taken += 1
                if size == ROWS:
                    top, bottom = top + extra[:HALF], bottom + extra[HALF:]
                elif at == 0:
                    top = top + extra
                else:
                    bottom = bottom + extra
            for out, at, start, size in puts:
                if size == ROWS:
                    outs[out][at : at + HALF, :] = top.astype(jnp.bfloat16)
                    outs[out][at + HALF : at + ROWS, :] = bottom.astype(jnp.bfloat16)
                else:
                    outs[out][at : at + HALF, :] = (top if start == 0 else bottom).astype(jnp.bfloat16)

    spec = lambda rows, k=0: pl.BlockSpec((rows, COLS), lambda n: (k, n))
    sources, source_specs = [], []
    for b, _, _ in blocks:
        sources += [mine, other]
        source_specs += [spec(CAP, b)] * 2
    return pl.pallas_call(
        kernel,
        grid=(width // COLS,),
        in_specs=[pl.BlockSpec(pos.shape, lambda n: (0, 0))] + source_specs + [spec(rows, k) for _, k, rows, _ in extras],
        out_specs=[spec(rows) for rows in sizes],
        out_shape=[jax.ShapeDtypeStruct((rows, width), jnp.bfloat16) for rows in sizes],
        compiler_params=params(20 * MIB),
        cost_estimate=SHORT,
    )(pos, *sources, *[a for a, _, _, _ in extras])


def routing(expert_ids, gate_weights, me, core, x, z):
    table = jnp.concatenate([expert_ids.T.astype(jnp.bfloat16), gate_weights.T], axis=0)
    table = jnp.concatenate([table, jnp.zeros((GATHERED - 16, ROWS), jnp.bfloat16)], axis=0)
    table = lax.all_gather(table, "expert", axis=0, tiled=False)[:, :16].reshape(SIDE, SIDE, 2, 16, ROWS)
    table = shifted(shifted(table, (x + 3) % SIDE, 0), (z + 3) % SIDE, 1)
    along_x, along_z = table[:, :, 0], jnp.swapaxes(table[:, :, 1], 0, 1)
    own = jnp.where(core == 0, along_x, along_z)
    partner = jnp.where(core == 0, along_z, along_x)
    table = jnp.stack([own, partner]).reshape(2, SIDE * SIDE, 16, ROWS)
    both = jnp.stack([me, me ^ 1]).astype(jnp.bfloat16)
    match = table[:, :, None, :8] == both[None, None, :, None, None]
    hit = jnp.any(match, axis=3)
    gate = jnp.sum(jnp.where(match[:, :, 0], table[:, :, 8:].astype(jnp.float32), 0.0), axis=2)
    before = (jnp.arange(ROWS)[:, None] < jnp.arange(ROWS)[None, :]).astype(jnp.bfloat16)
    rank = jnp.einsum("abet,ts->abes", hit.astype(jnp.bfloat16), before, preferred_element_type=jnp.float32)
    slot = jnp.where(hit, rank.astype(jnp.int32), -1)
    is_slot = slot[:, :, 0, None, :] == jnp.arange(CAP, dtype=jnp.int32)[None, None, :, None]
    gains = jnp.sum(jnp.where(is_slot, gate[:, :, None, :], 0.0), axis=3)
    return slot[0].reshape(SIDE, 2 * SIDE, ROWS), gains.reshape(2, SIDE, SIDE, CAP)


def together(*values):
    return lax.optimization_barrier(values)


def after(value, *others):
    return lax.optimization_barrier((value, *others))[0]


def passed(pos, *others):
    def kernel(pos_ref, *refs):
        refs[-1][...] = pos_ref[...]

    return pl.pallas_call(
        kernel,
        in_specs=[pl.BlockSpec(memory_space=pltpu.VMEM)] + [pl.BlockSpec(memory_space=pl.ANY)] * len(others),
        out_specs=pl.BlockSpec(memory_space=pltpu.VMEM),
        out_shape=jax.ShapeDtypeStruct(pos.shape, pos.dtype),
        compiler_params=params(MIB),
        cost_estimate=LONG,
    )(pos, *others)


def both_ways(to_right, to_left, second):
    return hop(to_right, 1, second), hop(to_left, -1, second)


def onward(left, right, way, second):
    return hop(left if way > 0 else right, way, second)


WAY_OUT = {0: -1, 1: -1, 2: 1, -1: 1}
WAY_BACK = {0: 1, 1: -1, 2: 1, -1: -1}


def on_device(tokens, expert_ids, gate_weights, expert_in, expert_out):
    me = lax.axis_index("expert")
    core, x, z = me % 2, me // 8, (me // 2) % 4
    first_weights, second_weights = expert_in[0], expert_out[0]
    whole = [(0, 0, 0, ROWS)]
    pos, mine, arrived, gain, outs, back, sent, got, last = {}, {}, {}, {}, {}, {}, {}, {}, []

    def ordered(value):
        return after(value, *last) if last else value

    def done(*values):
        last[:] = values
        return values

    def select(*group):
        arrays, places = [], []
        for k, i in enumerate(group):
            left, right, far = around[i]
            arrays += [left, along[i], right, far]
            places += [[(4 * k + n, 0, 0, ROWS)] for n in range(4)]
        slots = jnp.concatenate([slot[i + 1] for i in group], axis=0)
        mine[group], other = done(*select_rows(ordered(slots), places, arrays))
        pos[group], arrived[group] = slots.T, swap(other)
        gain[group] = jnp.concatenate([gains[side, i + 1] for side in (0, 1) for i in group], axis=0).reshape(-1, 1)

    def run(*group):
        mine[group] = ordered(mine[group])
        outs[group], other = done(*expert_rows(mine[group], arrived[group], gain[group], first_weights, second_weights))
        back[group] = swap(other)

    def spread(group, blocks, sizes):
        return done(*spread_rows(ordered(pos[group]), outs[group], back[group], blocks, sizes))

    def wait(*group, until):
        pos[group] = passed(pos[group], *until)

    def send_far(*group):
        parts = spread(group, [(4 * k + 3, [], [(k, 0, 0, ROWS)]) for k in range(len(group))], [ROWS] * len(group))
        for i, part in zip(group, parts):
            sent[i] = hop(part, WAY_BACK[i], True)

    def halves(group, place, extras):
        addends = [(e, 0, ROWS, 0) for e in extras]
        return spread(group, [(place, addends, [(0, 0, 0, HALF), (1, 0, HALF, HALF)])], [HALF, HALF])

    def send_near(group, i):
        place = 4 * group.index(i)
        if isinstance(sent[i], tuple):
            extras = [(sent[i][0], 0, HALF, 0)], [(sent[i][1], 0, HALF, HALF)]
        else:
            extra = [(sent[i], 0, ROWS, 0)]
            extras = (extra, []) if WAY_BACK[i] > 0 else ([], extra)
        blocks = [(place + 2, extras[0], whole), (place, extras[1], [(1, 0, 0, ROWS)])]
        got[i] = both_ways(*spread(group, blocks, [ROWS, ROWS]), True)

    def total(group, i, *extras):
        addends = [(e, 0, ROWS, 0) for e in got[i]] + [(e, 0, e.shape[0], at) for e, at in extras]
        return spread(group, [(4 * group.index(i) + 1, addends, whole)], [ROWS])[0]

    left, right = both_ways(tokens, tokens, False)
    near = {0: both_ways(tokens, tokens, True)}
    slot, gains = routing(expert_ids, gate_weights, me, core, x, z)
    left, right, *near[0] = together(left, right, *near[0])
    far = onward(left, right, 1, False)
    far0 = onward(*near[0], WAY_OUT[0], True)
    near[1], near[-1] = both_ways(right, right, True), both_ways(left, left, True)
    far, far0 = together(far, far0)
    near[2] = both_ways(far, far, True)
    along = {0: tokens, 1: right, 2: far, -1: left}
    around = {0: (*near[0], far0)}
    first, middle, final = (0,), (1, 2), (-1,)
    select(*first)
    run(*first)
    for i in (1, 2, -1):
        around[i] = (*near[i], onward(*near[i], WAY_OUT[i], True))
    wait(*first, until=(*near[1], *near[-1]))
    send_far(*first)
    select(*middle)
    run(*middle)
    wait(*middle, until=(sent[0], around[-1][2]))
    select(*final)
    send_far(*middle)
    send_near(first, 0)
    run(*final)
    wait(*final, until=(*got[0], sent[1], sent[2]))
    send_near(middle, 2)
    send_near(middle, 1)
    sent[-1] = both_ways(*halves(final, 3, ()), True)
    from_left, from_right = both_ways(*halves(middle, 5, got[2]), False)
    send_near(final, -1)
    to_right = hop(total(middle, 1, (from_left, 0)), 1, False)
    to_left = hop(total(final, -1, (from_right, HALF)), -1, False)
    return total(first, 0, (to_right, 0), (to_left, 0))


def solution(mesh):
    placed = (
        P(("dp", "expert"), None),
        P(("dp", "expert"), None),
        P(("dp", "expert"), None),
        P("expert", None, None),
        P("expert", None, None),
    )
    return jax.shard_map(
        on_device, mesh=mesh, in_specs=placed, out_specs=P(("dp", "expert"), None), check_vma=False
    )
```

```python
import jax
import jax.numpy as jnp
from jax import lax
from jax.experimental import pallas as pl
from jax.experimental.pallas import tpu as pltpu
from jax.sharding import PartitionSpec as P

SIDE = 4
CAP = 48
ROWS = 128
HALF = 64
COLS = 2048
NT = 1024
GATHERED = 128
FT = 256
MIB = 1024 * 1024


def chip_index(x, z, core):
    return (x % SIDE) * (2 * SIDE) + (z % SIDE) * 2 + core


def ring_pairs(step, second):
    pairs = []
    for i in range(2 * SIDE * SIDE):
        x, z, core = i // 8, (i // 2) % 4, i % 2
        along_x = (core == 0) != second
        pairs.append((i, chip_index(x + step, z, core) if along_x else chip_index(x, z + step, core)))
    return pairs


SWAP = [(i, i ^ 1) for i in range(2 * SIDE * SIDE)]


def hop(value, step, second):
    return lax.ppermute(value, "expert", ring_pairs(step, second))


def swap(value):
    return lax.ppermute(value, "expert", SWAP)


def shifted(table, start, axis):
    return lax.dynamic_slice_in_dim(jnp.concatenate([table, table], axis=axis), start, SIDE, axis)


SHORT = pl.CostEstimate(flops=1000, bytes_accessed=1000, transcendentals=0)


LONG = pl.CostEstimate(flops=10**12, bytes_accessed=10**9, transcendentals=0)


def params(vmem):
    return pltpu.CompilerParams(vmem_limit_bytes=vmem)


def select_rows(pos, places, arrays):
    width = arrays[0].shape[1]
    count = len(places) * CAP

    def kernel(pos_ref, *refs):
        arrays, (mine_ref, other_ref) = refs[:-2], refs[-2:]
        slots = lax.broadcasted_iota(jnp.int32, (2 * CAP, ROWS), 0)
        for b, parts in enumerate(places):
            first, second = pos_ref[2 * b : 2 * b + 1, :], pos_ref[2 * b + 1 : 2 * b + 2, :]
            slot = jnp.where(slots < CAP, first, jnp.where(second < 0, -1, second + CAP))
            pick = jnp.where(slot == slots, 1.0, 0.0).astype(jnp.bfloat16)
            rows = None
            for n, start, at, size in parts:
                part = jnp.dot(pick[:, at : at + size], arrays[n][start : start + size, :], preferred_element_type=jnp.float32)
                rows = part if rows is None else rows + part
            mine_ref[b * CAP : (b + 1) * CAP, :] = rows[:CAP].astype(jnp.bfloat16)
            other_ref[b * CAP : (b + 1) * CAP, :] = rows[CAP:].astype(jnp.bfloat16)

    spec = lambda rows: pl.BlockSpec((rows, COLS), lambda n: (0, n))
    out = jax.ShapeDtypeStruct((count, width), jnp.bfloat16)
    return pl.pallas_call(
        kernel,
        grid=(width // COLS,),
        in_specs=[pl.BlockSpec(pos.shape, lambda n: (0, 0))] + [spec(a.shape[0]) for a in arrays],
        out_specs=[spec(count)] * 2,
        out_shape=[out, out],
        compiler_params=params(24 * MIB),
        cost_estimate=SHORT,
    )(pos, *arrays)


def expert_kernel(steps, mine_ref, other_ref, gain_ref, gate_ref, up_ref, down_ref, mine_out, other_out, rows_ref, act_ref):
    step = pl.program_id(0)
    half = mine_ref.shape[0]

    @pl.when(step == 0)
    def _():
        rows_ref[:half, :] = mine_ref[...]
        rows_ref[half:, :] = other_ref[...]

    for f in range(steps):

        @pl.when(step == f)
        def _():
            rows = rows_ref[...]
            first = jnp.dot(rows, gate_ref[...], preferred_element_type=jnp.float32)
            second = jnp.dot(rows, up_ref[...], preferred_element_type=jnp.float32)
            act_ref[:, f * FT : (f + 1) * FT] = (first / (1.0 + jnp.exp(-first)) * second).astype(jnp.bfloat16)

    @pl.when(step >= steps)
    def _():
        part = jnp.dot(act_ref[...], down_ref[...], preferred_element_type=jnp.float32)
        weighted = (part * gain_ref[...]).astype(jnp.bfloat16)
        mine_out[...] = weighted[:half]
        other_out[...] = weighted[half:]


def expert_rows(mine, other, gains, expert_in, expert_out):
    count, width = mine.shape
    hidden = expert_out.shape[0]
    steps = hidden // FT
    whole = pl.BlockSpec((count, width), lambda s: (0, 0), pipeline_mode=pl.Buffered(1))
    columns = 2 * NT if count == 4 * CAP else NT
    late = lambda s: jnp.maximum(s - steps, 0)
    early = lambda s: jnp.minimum(s, steps - 1)
    out = jax.ShapeDtypeStruct((count, width), jnp.bfloat16)

    def body(*refs):
        expert_kernel(steps, *refs)

    return pl.pallas_call(
        body,
        grid=(steps + width // columns,),
        in_specs=[
            whole,
            whole,
            pl.BlockSpec((2 * count, 1), lambda s: (0, 0)),
            pl.BlockSpec((width, FT), lambda s: (0, early(s))),
            pl.BlockSpec((width, FT), lambda s: (0, early(s) + steps)),
            pl.BlockSpec((hidden, columns), lambda s: (0, late(s))),
        ],
        out_specs=[pl.BlockSpec((count, columns), lambda s: (0, late(s)))] * 2,
        out_shape=[out, out],
        scratch_shapes=[
            pltpu.VMEM((2 * count, width), jnp.bfloat16),
            pltpu.VMEM((2 * count, hidden), jnp.bfloat16),
        ],
        compiler_params=params(44 * MIB),
        cost_estimate=SHORT,
    )(mine, other, gains, expert_in, expert_in, expert_out)


def spread_rows(pos, mine, other, blocks, sizes):
    width = mine.shape[1]
    extras = [addend for _, addends, _ in blocks for addend in addends]
    plan = [(b, [(rows, at) for _, _, rows, at in addends], puts) for b, addends, puts in blocks]

    def kernel(pos_ref, *refs):
        slots = lax.broadcasted_iota(jnp.int32, (ROWS, 2 * CAP), 1)
        sources, refs = refs[: 2 * len(plan)], refs[2 * len(plan) :]
        extra_refs, outs = refs[: len(extras)], refs[len(extras) :]
        taken = 0
        for n, (b, addends, puts) in enumerate(plan):
            first, second = pos_ref[:, 2 * b : 2 * b + 1], pos_ref[:, 2 * b + 1 : 2 * b + 2]
            slot = jnp.where(slots < CAP, first, jnp.where(second < 0, -1, second + CAP))
            put = jnp.where(slot == slots, 1.0, 0.0).astype(jnp.bfloat16)
            rows = jnp.concatenate([sources[2 * n][...], sources[2 * n + 1][...]], axis=0)
            total = jnp.dot(put, rows, preferred_element_type=jnp.float32)
            top, bottom = total[:HALF], total[HALF:]
            for size, at in addends:
                extra = extra_refs[taken][...].astype(jnp.float32)
                taken += 1
                if size == ROWS:
                    top, bottom = top + extra[:HALF], bottom + extra[HALF:]
                elif at == 0:
                    top = top + extra
                else:
                    bottom = bottom + extra
            for out, at, start, size in puts:
                if size == ROWS:
                    outs[out][at : at + HALF, :] = top.astype(jnp.bfloat16)
                    outs[out][at + HALF : at + ROWS, :] = bottom.astype(jnp.bfloat16)
                else:
                    outs[out][at : at + HALF, :] = (top if start == 0 else bottom).astype(jnp.bfloat16)

    spec = lambda rows, k=0: pl.BlockSpec((rows, COLS), lambda n: (k, n))
    sources, source_specs = [], []
    for b, _, _ in blocks:
        sources += [mine, other]
        source_specs += [spec(CAP, b)] * 2
    return pl.pallas_call(
        kernel,
        grid=(width // COLS,),
        in_specs=[pl.BlockSpec(pos.shape, lambda n: (0, 0))] + source_specs + [spec(rows, k) for _, k, rows, _ in extras],
        out_specs=[spec(rows) for rows in sizes],
        out_shape=[jax.ShapeDtypeStruct((rows, width), jnp.bfloat16) for rows in sizes],
        compiler_params=params(20 * MIB),
        cost_estimate=SHORT,
    )(pos, *sources, *[a for a, _, _, _ in extras])


def routing(expert_ids, gate_weights, me, core, x, z):
    table = jnp.concatenate([expert_ids.T.astype(jnp.bfloat16), gate_weights.T], axis=0)
    table = jnp.concatenate([table, jnp.zeros((GATHERED - 16, ROWS), jnp.bfloat16)], axis=0)
    table = lax.all_gather(table, "expert", axis=0, tiled=False)[:, :16].reshape(SIDE, SIDE, 2, 16, ROWS)
    table = shifted(shifted(table, (x + 3) % SIDE, 0), (z + 3) % SIDE, 1)
    along_x, along_z = table[:, :, 0], jnp.swapaxes(table[:, :, 1], 0, 1)
    own = jnp.where(core == 0, along_x, along_z)
    partner = jnp.where(core == 0, along_z, along_x)
    table = jnp.stack([own, partner]).reshape(2, SIDE * SIDE, 16, ROWS)
    both = jnp.stack([me, me ^ 1]).astype(jnp.bfloat16)
    match = table[:, :, None, :8] == both[None, None, :, None, None]
    hit = jnp.any(match, axis=3)
    gate = jnp.sum(jnp.where(match[:, :, 0], table[:, :, 8:].astype(jnp.float32), 0.0), axis=2)
    before = (jnp.arange(ROWS)[:, None] < jnp.arange(ROWS)[None, :]).astype(jnp.bfloat16)
    rank = jnp.einsum("abet,ts->abes", hit.astype(jnp.bfloat16), before, preferred_element_type=jnp.float32)
    slot = jnp.where(hit, rank.astype(jnp.int32), -1)
    is_slot = slot[:, :, 0, None, :] == jnp.arange(CAP, dtype=jnp.int32)[None, None, :, None]
    gains = jnp.sum(jnp.where(is_slot, gate[:, :, None, :], 0.0), axis=3)
    return slot[0].reshape(SIDE, 2 * SIDE, ROWS), gains.reshape(2, SIDE, SIDE, CAP)


def together(*values):
    return lax.optimization_barrier(values)


def after(value, *others):
    return lax.optimization_barrier((value, *others))[0]


def passed(pos, *others):
    def kernel(pos_ref, *refs):
        refs[-1][...] = pos_ref[...]

    return pl.pallas_call(
        kernel,
        in_specs=[pl.BlockSpec(memory_space=pltpu.VMEM)] + [pl.BlockSpec(memory_space=pl.ANY)] * len(others),
        out_specs=pl.BlockSpec(memory_space=pltpu.VMEM),
        out_shape=jax.ShapeDtypeStruct(pos.shape, pos.dtype),
        compiler_params=params(MIB),
        cost_estimate=LONG,
    )(pos, *others)


def both_ways(to_right, to_left, second):
    return hop(to_right, 1, second), hop(to_left, -1, second)


def onward(left, right, way, second):
    return hop(left if way > 0 else right, way, second)


WAY_OUT = {0: -1, 1: -1, 2: 1, -1: 1}
WAY_BACK = {0: 1, 1: -1, 2: 1, -1: -1}


def on_device(tokens, expert_ids, gate_weights, expert_in, expert_out):
    me = lax.axis_index("expert")
    core, x, z = me % 2, me // 8, (me // 2) % 4
    first_weights, second_weights = expert_in[0], expert_out[0]
    whole = [(0, 0, 0, ROWS)]
    pos, mine, arrived, gain, outs, back, sent, got, last = {}, {}, {}, {}, {}, {}, {}, {}, []

    def ordered(value):
        return after(value, *last) if last else value

    def done(*values):
        last[:] = values
        return values

    def select(*group):
        arrays, places = [], []
        for k, i in enumerate(group):
            left, right, far = around[i]
            arrays += [left, along[i], right, far]
            places += [[(4 * k + n, 0, 0, ROWS)] for n in range(4)]
        slots = jnp.concatenate([slot[i + 1] for i in group], axis=0)
        mine[group], other = done(*select_rows(ordered(slots), places, arrays))
        pos[group], arrived[group] = slots.T, swap(other)
        gain[group] = jnp.concatenate([gains[side, i + 1] for side in (0, 1) for i in group], axis=0).reshape(-1, 1)

    def run(*group):
        mine[group] = ordered(mine[group])
        outs[group], other = done(*expert_rows(mine[group], arrived[group], gain[group], first_weights, second_weights))
        back[group] = swap(other)

    def spread(group, blocks, sizes):
        return done(*spread_rows(ordered(pos[group]), outs[group], back[group], blocks, sizes))

    def wait(*group, until):
        pos[group] = passed(pos[group], *until)

    def send_far(*group):
        parts = spread(group, [(4 * k + 3, [], [(k, 0, 0, ROWS)]) for k in range(len(group))], [ROWS] * len(group))
        for i, part in zip(group, parts):
            sent[i] = hop(part, WAY_BACK[i], True)

    def halves(group, place, extras):
        addends = [(e, 0, ROWS, 0) for e in extras]
        return spread(group, [(place, addends, [(0, 0, 0, HALF), (1, 0, HALF, HALF)])], [HALF, HALF])

    def send_near(group, i):
        place = 4 * group.index(i)
        if isinstance(sent[i], tuple):
            extras = [(sent[i][0], 0, HALF, 0)], [(sent[i][1], 0, HALF, HALF)]
        else:
            extra = [(sent[i], 0, ROWS, 0)]
            extras = (extra, []) if WAY_BACK[i] > 0 else ([], extra)
        blocks = [(place + 2, extras[0], whole), (place, extras[1], [(1, 0, 0, ROWS)])]
        got[i] = both_ways(*spread(group, blocks, [ROWS, ROWS]), True)

    def total(group, i, *extras):
        addends = [(e, 0, ROWS, 0) for e in got[i]] + [(e, 0, e.shape[0], at) for e, at in extras]
        return spread(group, [(4 * group.index(i) + 1, addends, whole)], [ROWS])[0]

    left, right = both_ways(tokens, tokens, False)
    near = {0: both_ways(tokens, tokens, True)}
    slot, gains = routing(expert_ids, gate_weights, me, core, x, z)
    left, right = together(left, right)
    near[0] = together(*near[0])
    far = onward(left, right, 1, False)
    far0 = onward(*near[0], WAY_OUT[0], True)
    near[1], near[-1] = both_ways(right, right, True), both_ways(left, left, True)
    far, far0 = together(far, far0)
    near[2] = both_ways(far, far, True)
    along = {0: tokens, 1: right, 2: far, -1: left}
    around = {0: (*near[0], far0)}
    first, middle, final = (0,), (1, 2), (-1,)
    select(*first)
    run(*first)
    for i in (1, 2, -1):
        around[i] = (*near[i], onward(*near[i], WAY_OUT[i], True))
    wait(*first, until=(*near[1], *near[-1]))
    send_far(*first)
    select(*middle)
    run(*middle)
    wait(*middle, until=(sent[0], around[-1][2]))
    select(*final)
    send_far(*middle)
    run(*final)
    wait(*final, until=(sent[1], sent[2]))
    send_near(middle, 2)
    send_near(middle, 1)
    sent[-1] = both_ways(*halves(final, 3, ()), True)
    send_near(first, 0)
    from_left, from_right = both_ways(*halves(middle, 5, got[2]), False)
    send_near(final, -1)
    to_right = hop(total(middle, 1, (from_left, 0)), 1, False)
    to_left = hop(total(final, -1, (from_right, HALF)), -1, False)
    return total(first, 0, (to_right, 0), (to_left, 0))


def solution(mesh):
    placed = (
        P(("dp", "expert"), None),
        P(("dp", "expert"), None),
        P(("dp", "expert"), None),
        P("expert", None, None),
        P("expert", None, None),
    )
    return jax.shard_map(
        on_device, mesh=mesh, in_specs=placed, out_specs=P(("dp", "expert"), None), check_vma=False
    )
```

```python
import jax
import jax.numpy as jnp
from jax import lax
from jax.experimental import pallas as pl
from jax.experimental.pallas import tpu as pltpu
from jax.sharding import PartitionSpec as P

SIDE = 4
CAP = 48
ROWS = 128
HALF = 64
COLS = 2048
NT = 1024
GATHERED = 128
FT = 256
MIB = 1024 * 1024


def chip_index(x, z, core):
    return (x % SIDE) * (2 * SIDE) + (z % SIDE) * 2 + core


def ring_pairs(step, second):
    pairs = []
    for i in range(2 * SIDE * SIDE):
        x, z, core = i // 8, (i // 2) % 4, i % 2
        along_x = (core == 0) != second
        pairs.append((i, chip_index(x + step, z, core) if along_x else chip_index(x, z + step, core)))
    return pairs


SWAP = [(i, i ^ 1) for i in range(2 * SIDE * SIDE)]


def hop(value, step, second):
    return lax.ppermute(value, "expert", ring_pairs(step, second))


def swap(value):
    return lax.ppermute(value, "expert", SWAP)


def shifted(table, start, axis):
    return lax.dynamic_slice_in_dim(jnp.concatenate([table, table], axis=axis), start, SIDE, axis)


SHORT = pl.CostEstimate(flops=1000, bytes_accessed=1000, transcendentals=0)


LONG = pl.CostEstimate(flops=10**12, bytes_accessed=10**9, transcendentals=0)


def params(vmem):
    return pltpu.CompilerParams(vmem_limit_bytes=vmem)


def select_rows(pos, places, arrays):
    width = arrays[0].shape[1]
    count = len(places) * CAP

    def kernel(pos_ref, *refs):
        arrays, (mine_ref, other_ref) = refs[:-2], refs[-2:]
        slots = lax.broadcasted_iota(jnp.int32, (2 * CAP, ROWS), 0)
        for b, parts in enumerate(places):
            first, second = pos_ref[2 * b : 2 * b + 1, :], pos_ref[2 * b + 1 : 2 * b + 2, :]
            slot = jnp.where(slots < CAP, first, jnp.where(second < 0, -1, second + CAP))
            pick = jnp.where(slot == slots, 1.0, 0.0).astype(jnp.bfloat16)
            rows = None
            for n, start, at, size in parts:
                part = jnp.dot(pick[:, at : at + size], arrays[n][start : start + size, :], preferred_element_type=jnp.float32)
                rows = part if rows is None else rows + part
            mine_ref[b * CAP : (b + 1) * CAP, :] = rows[:CAP].astype(jnp.bfloat16)
            other_ref[b * CAP : (b + 1) * CAP, :] = rows[CAP:].astype(jnp.bfloat16)

    spec = lambda rows: pl.BlockSpec((rows, COLS), lambda n: (0, n))
    out = jax.ShapeDtypeStruct((count, width), jnp.bfloat16)
    return pl.pallas_call(
        kernel,
        grid=(width // COLS,),
        in_specs=[pl.BlockSpec(pos.shape, lambda n: (0, 0))] + [spec(a.shape[0]) for a in arrays],
        out_specs=[spec(count)] * 2,
        out_shape=[out, out],
        compiler_params=params(24 * MIB),
        cost_estimate=SHORT,
    )(pos, *arrays)


def expert_kernel(steps, mine_ref, other_ref, gain_ref, gate_ref, up_ref, down_ref, mine_out, other_out, rows_ref, act_ref):
    step = pl.program_id(0)
    half = mine_ref.shape[0]

    @pl.when(step == 0)
    def _():
        rows_ref[:half, :] = mine_ref[...]
        rows_ref[half:, :] = other_ref[...]

    for f in range(steps):

        @pl.when(step == f)
        def _():
            rows = rows_ref[...]
            first = jnp.dot(rows, gate_ref[...], preferred_element_type=jnp.float32)
            second = jnp.dot(rows, up_ref[...], preferred_element_type=jnp.float32)
            act_ref[:, f * FT : (f + 1) * FT] = (first / (1.0 + jnp.exp(-first)) * second).astype(jnp.bfloat16)

    @pl.when(step >= steps)
    def _():
        part = jnp.dot(act_ref[...], down_ref[...], preferred_element_type=jnp.float32)
        weighted = (part * gain_ref[...]).astype(jnp.bfloat16)
        mine_out[...] = weighted[:half]
        other_out[...] = weighted[half:]


def expert_rows(mine, other, gains, expert_in, expert_out):
    count, width = mine.shape
    hidden = expert_out.shape[0]
    steps = hidden // FT
    whole = pl.BlockSpec((count, width), lambda s: (0, 0), pipeline_mode=pl.Buffered(1))
    columns = 2 * NT if count == 4 * CAP else NT
    late = lambda s: jnp.maximum(s - steps, 0)
    early = lambda s: jnp.minimum(s, steps - 1)
    out = jax.ShapeDtypeStruct((count, width), jnp.bfloat16)

    def body(*refs):
        expert_kernel(steps, *refs)

    return pl.pallas_call(
        body,
        grid=(steps + width // columns,),
        in_specs=[
            whole,
            whole,
            pl.BlockSpec((2 * count, 1), lambda s: (0, 0)),
            pl.BlockSpec((width, FT), lambda s: (0, early(s))),
            pl.BlockSpec((width, FT), lambda s: (0, early(s) + steps)),
            pl.BlockSpec((hidden, columns), lambda s: (0, late(s))),
        ],
        out_specs=[pl.BlockSpec((count, columns), lambda s: (0, late(s)))] * 2,
        out_shape=[out, out],
        scratch_shapes=[
            pltpu.VMEM((2 * count, width), jnp.bfloat16),
            pltpu.VMEM((2 * count, hidden), jnp.bfloat16),
        ],
        compiler_params=params(44 * MIB),
        cost_estimate=SHORT,
    )(mine, other, gains, expert_in, expert_in, expert_out)


def spread_rows(pos, mine, other, blocks, sizes):
    width = mine.shape[1]
    extras = [addend for _, addends, _ in blocks for addend in addends]
    plan = [(b, [(rows, at) for _, _, rows, at in addends], puts) for b, addends, puts in blocks]

    def kernel(pos_ref, *refs):
        slots = lax.broadcasted_iota(jnp.int32, (ROWS, 2 * CAP), 1)
        sources, refs = refs[: 2 * len(plan)], refs[2 * len(plan) :]
        extra_refs, outs = refs[: len(extras)], refs[len(extras) :]
        taken = 0
        for n, (b, addends, puts) in enumerate(plan):
            first, second = pos_ref[:, 2 * b : 2 * b + 1], pos_ref[:, 2 * b + 1 : 2 * b + 2]
            slot = jnp.where(slots < CAP, first, jnp.where(second < 0, -1, second + CAP))
            put = jnp.where(slot == slots, 1.0, 0.0).astype(jnp.bfloat16)
            rows = jnp.concatenate([sources[2 * n][...], sources[2 * n + 1][...]], axis=0)
            total = jnp.dot(put, rows, preferred_element_type=jnp.float32)
            top, bottom = total[:HALF], total[HALF:]
            for size, at in addends:
                extra = extra_refs[taken][...].astype(jnp.float32)
                taken += 1
                if size == ROWS:
                    top, bottom = top + extra[:HALF], bottom + extra[HALF:]
                elif at == 0:
                    top = top + extra
                else:
                    bottom = bottom + extra
            for out, at, start, size in puts:
                if size == ROWS:
                    outs[out][at : at + HALF, :] = top.astype(jnp.bfloat16)
                    outs[out][at + HALF : at + ROWS, :] = bottom.astype(jnp.bfloat16)
                else:
                    outs[out][at : at + HALF, :] = (top if start == 0 else bottom).astype(jnp.bfloat16)

    spec = lambda rows, k=0: pl.BlockSpec((rows, COLS), lambda n: (k, n))
    sources, source_specs = [], []
    for b, _, _ in blocks:
        sources += [mine, other]
        source_specs += [spec(CAP, b)] * 2
    return pl.pallas_call(
        kernel,
        grid=(width // COLS,),
        in_specs=[pl.BlockSpec(pos.shape, lambda n: (0, 0))] + source_specs + [spec(rows, k) for _, k, rows, _ in extras],
        out_specs=[spec(rows) for rows in sizes],
        out_shape=[jax.ShapeDtypeStruct((rows, width), jnp.bfloat16) for rows in sizes],
        compiler_params=params(20 * MIB),
        cost_estimate=SHORT,
    )(pos, *sources, *[a for a, _, _, _ in extras])


def routing(expert_ids, gate_weights, me, core, x, z):
    table = jnp.concatenate([expert_ids.T.astype(jnp.bfloat16), gate_weights.T], axis=0)
    table = jnp.concatenate([table, jnp.zeros((GATHERED - 16, ROWS), jnp.bfloat16)], axis=0)
    table = lax.all_gather(table, "expert", axis=0, tiled=False)[:, :16].reshape(SIDE, SIDE, 2, 16, ROWS)
    table = shifted(shifted(table, (x + 3) % SIDE, 0), (z + 3) % SIDE, 1)
    along_x, along_z = table[:, :, 0], jnp.swapaxes(table[:, :, 1], 0, 1)
    own = jnp.where(core == 0, along_x, along_z)
    partner = jnp.where(core == 0, along_z, along_x)
    table = jnp.stack([own, partner]).reshape(2, SIDE * SIDE, 16, ROWS)
    both = jnp.stack([me, me ^ 1]).astype(jnp.bfloat16)
    match = table[:, :, None, :8] == both[None, None, :, None, None]
    hit = jnp.any(match, axis=3)
    gate = jnp.sum(jnp.where(match[:, :, 0], table[:, :, 8:].astype(jnp.float32), 0.0), axis=2)
    before = (jnp.arange(ROWS)[:, None] < jnp.arange(ROWS)[None, :]).astype(jnp.bfloat16)
    rank = jnp.einsum("abet,ts->abes", hit.astype(jnp.bfloat16), before, preferred_element_type=jnp.float32)
    slot = jnp.where(hit, rank.astype(jnp.int32), -1)
    is_slot = slot[:, :, 0, None, :] == jnp.arange(CAP, dtype=jnp.int32)[None, None, :, None]
    gains = jnp.sum(jnp.where(is_slot, gate[:, :, None, :], 0.0), axis=3)
    return slot[0].reshape(SIDE, 2 * SIDE, ROWS), gains.reshape(2, SIDE, SIDE, CAP)


def together(*values):
    return lax.optimization_barrier(values)


def after(value, *others):
    return lax.optimization_barrier((value, *others))[0]


def passed(pos, *others):
    def kernel(pos_ref, *refs):
        refs[-1][...] = pos_ref[...]

    return pl.pallas_call(
        kernel,
        in_specs=[pl.BlockSpec(memory_space=pltpu.VMEM)] + [pl.BlockSpec(memory_space=pl.ANY)] * len(others),
        out_specs=pl.BlockSpec(memory_space=pltpu.VMEM),
        out_shape=jax.ShapeDtypeStruct(pos.shape, pos.dtype),
        compiler_params=params(MIB),
        cost_estimate=LONG,
    )(pos, *others)


def both_ways(to_right, to_left, second):
    return hop(to_right, 1, second), hop(to_left, -1, second)


def onward(left, right, way, second):
    return hop(left if way > 0 else right, way, second)


WAY_OUT = {0: -1, 1: -1, 2: 1, -1: 1}
WAY_BACK = {0: 1, 1: -1, 2: 1, -1: -1}


def on_device(tokens, expert_ids, gate_weights, expert_in, expert_out):
    me = lax.axis_index("expert")
    core, x, z = me % 2, me // 8, (me // 2) % 4
    first_weights, second_weights = expert_in[0], expert_out[0]
    whole = [(0, 0, 0, ROWS)]
    pos, mine, arrived, gain, outs, back, sent, got, last = {}, {}, {}, {}, {}, {}, {}, {}, []

    def ordered(value):
        return after(value, *last) if last else value

    def done(*values):
        last[:] = values
        return values

    def select(*group):
        arrays, places = [], []
        for k, i in enumerate(group):
            left, right, far = around[i]
            arrays += [left, along[i], right, far]
            places += [[(4 * k + n, 0, 0, ROWS)] for n in range(4)]
        slots = jnp.concatenate([slot[i + 1] for i in group], axis=0)
        mine[group], other = done(*select_rows(ordered(slots), places, arrays))
        pos[group], arrived[group] = slots.T, swap(other)
        gain[group] = jnp.concatenate([gains[side, i + 1] for side in (0, 1) for i in group], axis=0).reshape(-1, 1)

    def run(*group):
        mine[group] = ordered(mine[group])
        outs[group], other = done(*expert_rows(mine[group], arrived[group], gain[group], first_weights, second_weights))
        back[group] = swap(other)

    def spread(group, blocks, sizes):
        return done(*spread_rows(ordered(pos[group]), outs[group], back[group], blocks, sizes))

    def wait(*group, until):
        pos[group] = passed(pos[group], *until)

    def send_far(*group):
        parts = spread(group, [(4 * k + 3, [], [(k, 0, 0, ROWS)]) for k in range(len(group))], [ROWS] * len(group))
        for i, part in zip(group, parts):
            sent[i] = hop(part, WAY_BACK[i], True)

    def halves(group, place, extras):
        addends = [(e, 0, ROWS, 0) for e in extras]
        return spread(group, [(place, addends, [(0, 0, 0, HALF), (1, 0, HALF, HALF)])], [HALF, HALF])

    def send_near(group, i):
        place = 4 * group.index(i)
        if isinstance(sent[i], tuple):
            extras = [(sent[i][0], 0, HALF, 0)], [(sent[i][1], 0, HALF, HALF)]
        else:
            extra = [(sent[i], 0, ROWS, 0)]
            extras = (extra, []) if WAY_BACK[i] > 0 else ([], extra)
        blocks = [(place + 2, extras[0], whole), (place, extras[1], [(1, 0, 0, ROWS)])]
        got[i] = both_ways(*spread(group, blocks, [ROWS, ROWS]), True)

    def total(group, i, *extras):
        addends = [(e, 0, ROWS, 0) for e in got[i]] + [(e, 0, e.shape[0], at) for e, at in extras]
        return spread(group, [(4 * group.index(i) + 1, addends, whole)], [ROWS])[0]

    left, right = both_ways(tokens, tokens, False)
    near = {0: both_ways(tokens, tokens, True)}
    slot, gains = routing(expert_ids, gate_weights, me, core, x, z)
    left, right = together(left, right)
    near[0] = together(*near[0])
    far = onward(left, right, 1, False)
    far0 = onward(*near[0], WAY_OUT[0], True)
    near[1], near[-1] = both_ways(right, right, True), both_ways(left, left, True)
    far, far0 = together(far, far0)
    near[2] = both_ways(far, far, True)
    along = {0: tokens, 1: right, 2: far, -1: left}
    around = {0: (*near[0], far0)}
    first, middle, final = (0,), (1, 2), (-1,)
    select(*first)
    run(*first)
    for i in (1, 2, -1):
        around[i] = (*near[i], onward(*near[i], WAY_OUT[i], True))
    wait(*first, until=(*near[1], *near[-1]))
    send_far(*first)
    select(*middle)
    run(*middle)
    wait(*middle, until=(sent[0], around[-1][2]))
    select(*final)
    send_far(*middle)
    run(*final)
    wait(*final, until=(sent[1], sent[2]))
    send_near(middle, 2)
    sent[-1] = both_ways(*halves(final, 3, ()), True)
    from_left, from_right = both_ways(*halves(middle, 5, got[2]), False)
    send_near(middle, 1)
    send_near(final, -1)
    send_near(first, 0)
    to_right = hop(total(middle, 1, (from_left, 0)), 1, False)
    to_left = hop(total(final, -1, (from_right, HALF)), -1, False)
    return total(first, 0, (to_right, 0), (to_left, 0))


def solution(mesh):
    placed = (
        P(("dp", "expert"), None),
        P(("dp", "expert"), None),
        P(("dp", "expert"), None),
        P("expert", None, None),
        P("expert", None, None),
    )
    return jax.shard_map(
        on_device, mesh=mesh, in_specs=placed, out_specs=P(("dp", "expert"), None), check_vma=False
    )
```
